512 devices in a mesh: gx: 8 (over y, core), gy: 8 (over z_hi, x), gz: 8 (over z_lo).
Axes of the slice: x: 4, y: 4, z: 16 (z_hi: 2, z_lo: 8; z = z_hi * 8 + z_lo), core: 2. Of those that a mesh axis runs over, the one named last changes fastest.
Arguments:
- inputs: bfloat16 [1024, 12288], P(('gx', 'gz'), 'gy'), may hold values from -60 to 60
- ln_gain: float32 [12288], P('gy'), may hold values from 0.5 to 1.5
- ln_bias: float32 [12288], P('gy'), may hold values from -3 to 3
- weight_in: bfloat16 [12288, 24576], P(('gy', 'gx'), 'gz'), may hold values from -0.0546875 to 0.0546875
- up_bias: float32 [24576], P('gz'), may hold values from -3 to 3
- grad_hidden: bfloat16 [1024, 24576], P(('gx', 'gy'), 'gz'), may hold values from -24 to 24
Outputs:
- grad_inputs: bfloat16 [1024, 12288], P(('gx', 'gz'), 'gy')
- grad_weight: bfloat16 [12288, 24576], P(('gy', 'gx'), 'gz')
- grad_up_bias: float32 [24576], P('gz')
- grad_ln_gain: float32 [12288], P('gy')
- grad_ln_bias: float32 [12288], P('gy')
The draws below stay inside these ranges and needn't reach their ends.
All inputs are finite; a program needn't handle non-finite values.
Results may differ from the reference program's by a relative error of at most 0.019.
Values may be sent and summed in bfloat16 or wider, within the bound.
No kernel may reach another device: no remote copies, remote signals or barrier semaphores. Data moves between devices by JAX's collectives and lax.ppermute only.
A program may use at most 64 MiB of HBM per device.

```python
import math
import jax
import jax.numpy as jnp
from jax import lax

D = 12288
FF = 24576
TOKENS = 1024
N_GY = 8
N_GZ = 8


def draw_inputs(key, part):
    key = jax.random.fold_in(key, 11)
    key_base, key_rows, key_cols = jax.random.split(key, 3)
    row_scale = jnp.exp(jax.random.uniform(key_rows, (TOKENS, 1), jnp.float32) * math.log(10.0))
    col_scale = jnp.exp(jax.random.uniform(key_cols, (1, D), jnp.float32) * math.log(10.0))
    column = jnp.arange(D, dtype=jnp.float32).reshape(1, D) / max(D - 1, 1)
    base = jax.random.normal(key_base, (TOKENS, D), jnp.float32)
    offset = 1.0 + 2.0 * column
    value = (base * col_scale / 3.0 + offset) * row_scale
    return jnp.clip(value, -60.0, 60.0).astype(jnp.bfloat16)


def draw_grad_hidden(key, part):
    key = jax.random.fold_in(key, 23)
    key_base, key_rows = jax.random.split(key, 2)
    row_scale = jnp.exp(jax.random.uniform(key_rows, (TOKENS, 1), jnp.float32) * math.log(10.0))
    position = jnp.arange(TOKENS, dtype=jnp.float32).reshape(TOKENS, 1)
    ramp = 1.0 + 2.0 * position / max(TOKENS - 1, 1)
    base = jax.random.normal(key_base, (TOKENS, FF), jnp.float32)
    value = 0.1 * base * row_scale * ramp
    return jnp.clip(value, -24.0, 24.0).astype(jnp.bfloat16)


def levels(key, dims, cuts, low, high):
    gain, own = 1.0, jax.random.fold_in(key, 6)
    for axis_at, blocks in cuts:
        draws = jnp.exp(jax.random.uniform(jax.random.fold_in(own, axis_at), (blocks,), jnp.float32, low / len(cuts), high / len(cuts)))
        gain = gain * jnp.repeat(draws, dims[axis_at] // blocks).reshape([-1 if axis == axis_at else 1 for axis in range(len(dims))])
    return gain


def bell_draw(rng, extent, deviation, reach, shards=(), kind=jnp.bfloat16):
    result = deviation * jax.random.normal(rng, extent, jnp.float32)
    if shards:
        result = result * levels(rng, extent, shards, -0.22, 0.18)
    return jnp.clip(result, -reach, reach).astype(kind)


def setup_inputs(seed: int = 0) -> dict:
    key_of = jax.random.split(jax.random.key(seed), 7)
    return {
        "inputs": draw_inputs(jax.random.fold_in(key_of[6], 71), 0),
        "ln_gain": jnp.clip(1.0 + 0.1 * jax.random.normal(key_of[1], (D,), jnp.float32), 0.5, 1.5),
        "ln_bias": bell_draw(key_of[2], (D,), 0.5, 3.0, ((0, 8),), jnp.float32),
        "weight_in": bell_draw(key_of[3], (D, FF), D ** -0.5, 0.0546875, ((0, 64), (1, 8))),
        "up_bias": bell_draw(key_of[4], (FF,), 0.5, 3.0, ((0, 8),), jnp.float32),
        "grad_hidden": draw_grad_hidden(jax.random.fold_in(key_of[6], 71), 0),
    }


gelu_scale = math.sqrt(2.0 / math.pi)
cubic = 0.044715
epsilon = 1e-05

def gelu_slope(value):
    inner = gelu_scale * (value + cubic * value * value * value)
    tangent = jnp.tanh(inner)
    return 0.5 * (1.0 + tangent) + 0.5 * value * (1.0 - tangent * tangent) * gelu_scale * (1.0 + 3.0 * cubic * value * value)

def reference(inputs, ln_gain, ln_bias, weight_in, up_bias, grad_hidden):
    x_float = inputs.astype(jnp.float32)
    mean = lax.optimization_barrier(jnp.mean(x_float, axis=1, keepdims=True))
    centered = x_float - mean
    variance = lax.optimization_barrier(jnp.mean(centered * centered, axis=1, keepdims=True))
    inv_std = lax.rsqrt(variance + epsilon)
    x_hat = centered * inv_std
    normed = (x_hat * ln_gain + ln_bias).astype(jnp.bfloat16)
    block_width = D // N_GY
    hidden = jnp.zeros((TOKENS, FF), jnp.float32)
    for index in range(N_GY):
        part = jnp.dot(normed[:, index * block_width:(index + 1) * block_width], weight_in[index * block_width:(index + 1) * block_width], preferred_element_type=jnp.float32).astype(jnp.bfloat16)
        part = lax.optimization_barrier(part)
        hidden = hidden + part.astype(jnp.float32)
    hidden = hidden + up_bias
    grad_pre = (grad_hidden.astype(jnp.float32) * gelu_slope(hidden)).astype(jnp.bfloat16)
    grad_up_bias = lax.optimization_barrier(jnp.sum(grad_pre.astype(jnp.float32), axis=0))
    grad_weight = jnp.dot(normed.T, grad_pre, preferred_element_type=jnp.float32).astype(jnp.bfloat16)
    hidden_width = FF // N_GZ
    back_total = jnp.zeros((TOKENS, D), jnp.float32)
    for index in range(N_GZ):
        back = jnp.dot(grad_pre[:, index * hidden_width:(index + 1) * hidden_width], weight_in[:, index * hidden_width:(index + 1) * hidden_width].T, preferred_element_type=jnp.float32).astype(jnp.bfloat16)
        back = lax.optimization_barrier(back)
        back_total = back_total + back.astype(jnp.float32)
    grad_normed = back_total.astype(jnp.bfloat16)
    grad_float = grad_normed.astype(jnp.float32)
    scaled = grad_float * ln_gain
    first_mean = lax.optimization_barrier(jnp.mean(scaled, axis=1, keepdims=True))
    second_mean = lax.optimization_barrier(jnp.mean(scaled * x_hat, axis=1, keepdims=True))
    grad_inputs = (inv_std * (scaled - first_mean - x_hat * second_mean)).astype(jnp.bfloat16)
    grad_ln_gain = lax.optimization_barrier(jnp.sum(grad_float * x_hat, axis=0))
    grad_ln_bias = lax.optimization_barrier(jnp.sum(grad_float, axis=0))
    return (grad_inputs, grad_weight, grad_up_bias, grad_ln_gain, grad_ln_bias)
```

```python
import math

import jax
import jax.numpy as jnp
from jax import lax
from jax.sharding import Mesh, PartitionSpec as P

D = 12288


gelu_scale = math.sqrt(2.0 / math.pi)
cubic = 0.044715
epsilon = 1e-05

gx = ("y", "core")
gy = ("zh", "x")


def gelu_slope(value):
    inner = gelu_scale * (value + cubic * value * value * value)
    tangent = jnp.tanh(inner)
    return 0.5 * (1.0 + tangent) + 0.5 * value * (1.0 - tangent * tangent) * gelu_scale * (
        1.0 + 3.0 * cubic * value * value
    )


def exchange(blocks, axis):
    return lax.all_to_all(blocks, axis, split_axis=0, concat_axis=0, tiled=True)


def spread(block, axis):
    count = lax.axis_size(axis)
    return exchange(jnp.broadcast_to(block[None], (count,) + block.shape), axis)


def swap(block):
    return lax.ppermute(block, "zh", [(0, 1), (1, 0)])


def split_float(value):
    high = lax.reduce_precision(value, 8, 7)
    return high.astype(jnp.bfloat16), (value - high).astype(jnp.bfloat16)


def shards(inputs, ln_gain, ln_bias, weight_in, up_bias, grad_hidden):
    f32, bf16 = jnp.float32, jnp.bfloat16
    rows, width = inputs.shape
    hidden_width = weight_in.shape[1]
    sub_width = weight_in.shape[0]
    depth = lax.axis_size("gz")
    halves, around = lax.axis_size("zh"), lax.axis_size("x")
    local = depth * rows

    weight = lax.all_gather(weight_in, gx, axis=0, tiled=True)

    x_float = (
        spread(inputs, "gz")
        .reshape(halves, around, rows, width)
        .transpose(1, 0, 2, 3)
        .reshape(local, width)
        .astype(f32)
    )
    own_mean = jnp.mean(x_float, axis=1)
    own_centered = x_float - own_mean[:, None]
    own_square = jnp.sum(own_centered * own_centered, axis=1)
    moments = spread(jnp.stack([own_mean, own_square]), gy)
    mean = jnp.mean(moments[:, 0], axis=0)
    shift = moments[:, 0] - mean
    variance = (jnp.sum(moments[:, 1], axis=0) + width * jnp.sum(shift * shift, axis=0)) / D
    inv_std = lax.rsqrt(variance + epsilon)
    x_hat = (x_float - mean[:, None]) * inv_std[:, None]
    normed = (x_hat * ln_gain + ln_bias).astype(bf16)

    other_cotangent = swap(grad_hidden)
    upper = lax.axis_index("zh") == 1
    cotangent = jnp.concatenate(
        [
            jnp.where(upper, other_cotangent, grad_hidden),
            jnp.where(upper, grad_hidden, other_cotangent),
        ]
    ).astype(f32)

    partial_hidden = jnp.dot(normed, weight, preferred_element_type=f32).astype(bf16)
    arrived = exchange(partial_hidden.reshape(around, halves * rows, hidden_width), "x")
    half_sum = lax.reduce_precision(jnp.sum(arrived.astype(f32), axis=0), 8, 7)
    hidden = half_sum + swap(half_sum.astype(bf16)).astype(f32) + up_bias
    grad_pre = (cotangent * gelu_slope(hidden)).astype(bf16)
    grad_local = spread(grad_pre, "x").reshape(local, hidden_width)
    portion = lax.all_gather(grad_local, gx, axis=0, tiled=True)

    feature_rows = exchange(
        normed.reshape(local, width // sub_width, sub_width).transpose(1, 0, 2), gx
    ).reshape(-1, sub_width)
    grad_weight = lax.dot_general(
        feature_rows, portion, (((0,), (0,)), ((), ())), preferred_element_type=f32
    ).astype(bf16)
    grad_up_bias = jnp.sum(portion.astype(f32), axis=0)

    back = lax.dot_general(
        grad_local, weight, (((1,), (1,)), ((), ())), preferred_element_type=f32
    )
    sums = jnp.stack([jnp.sum(back * x_hat, axis=0), jnp.sum(back, axis=0)])
    high, low = split_float(sums)
    extra = jnp.concatenate([high, low, jnp.zeros((4, width), bf16)])
    ordered = (
        back.astype(bf16)
        .reshape(around, halves, rows, width)
        .transpose(1, 0, 2, 3)
        .reshape(depth, rows, width)
    )
    landed = exchange(
        jnp.concatenate([ordered, jnp.broadcast_to(extra[None], (depth,) + extra.shape)], axis=1),
        "gz",
    ).astype(f32)
    total = jnp.sum(landed, axis=0)
    grad_float = total[:rows].astype(bf16).astype(f32)
    depth_sums = total[rows : rows + 2] + total[rows + 2 : rows + 4]
    grad_ln_gain, grad_ln_bias = jnp.sum(spread(depth_sums, gx), axis=0)

    def mine(value):
        ordered = value.reshape(around, halves, rows).transpose(1, 0, 2).reshape(depth, rows)
        return lax.dynamic_index_in_dim(ordered, lax.axis_index("gz"), 0, keepdims=False)[:, None]

    own_inv = mine(inv_std)
    own_hat = (inputs.astype(f32) - mine(mean)) * own_inv
    scaled = grad_float * ln_gain
    token_sums = jnp.stack([jnp.sum(scaled, axis=1), jnp.sum(scaled * own_hat, axis=1)])
    first_total, second_total = jnp.sum(spread(token_sums, gy), axis=0)
    grad_inputs = (
        own_inv * (scaled - first_total[:, None] / D - own_hat * (second_total[:, None] / D))
    ).astype(bf16)
    return (grad_inputs, grad_weight, grad_up_bias, grad_ln_gain, grad_ln_bias)


def solution(mesh):
    cube = Mesh(mesh.devices.reshape(4, 2, 2, 4, 8), ("y", "core", "zh", "x", "gz"))
    return jax.shard_map(
        shards,
        mesh=cube,
        in_specs=(
            P(("y", "core", "gz"), gy),
            P(gy),
            P(gy),
            P(("zh", "x", "y", "core"), "gz"),
            P("gz"),
            P(("y", "core", "zh", "x"), "gz"),
        ),
        out_specs=(
            P(("y", "core", "gz"), gy),
            P(("zh", "x", "y", "core"), "gz"),
            P("gz"),
            P(gy),
            P(gy),
        ),
        check_vma=False,
    )
```

```python
import math

import jax
import jax.numpy as jnp
from jax import lax
from jax.sharding import Mesh, PartitionSpec as P

D = 12288


gelu_scale = math.sqrt(2.0 / math.pi)
cubic = 0.044715
epsilon = 1e-05

gx = ("y", "core")
gy = ("zh", "x")


def gelu_slope(value):
    inner = gelu_scale * (value + cubic * value * value * value)
    tangent = jnp.tanh(inner)
    return 0.5 * (1.0 + tangent) + 0.5 * value * (1.0 - tangent * tangent) * gelu_scale * (
        1.0 + 3.0 * cubic * value * value
    )


def exchange(blocks, axis):
    return lax.all_to_all(blocks, axis, split_axis=0, concat_axis=0, tiled=True)


def spread(block, axis):
    count = lax.axis_size(axis)
    return exchange(jnp.broadcast_to(block[None], (count,) + block.shape), axis)


def swap(block):
    return lax.ppermute(block, "zh", [(0, 1), (1, 0)])


def shards(inputs, ln_gain, ln_bias, weight_in, up_bias, grad_hidden):
    f32, bf16 = jnp.float32, jnp.bfloat16
    rows, width = inputs.shape
    hidden_width = weight_in.shape[1]
    sub_width = weight_in.shape[0]
    depth = lax.axis_size("gz")
    halves, around = lax.axis_size("zh"), lax.axis_size("x")
    local = depth * rows

    weight = lax.all_gather(weight_in, gx, axis=0, tiled=True)

    x_float = (
        spread(inputs, "gz")
        .reshape(halves, around, rows, width)
        .transpose(1, 0, 2, 3)
        .reshape(local, width)
        .astype(f32)
    )
    own_mean = jnp.mean(x_float, axis=1)
    own_centered = x_float - own_mean[:, None]
    own_square = jnp.sum(own_centered * own_centered, axis=1)
    other_cotangent = swap(grad_hidden)
    own_square = own_square + 0.0 * other_cotangent[0, 0].astype(f32)
    moments = spread(jnp.stack([own_mean, own_square]), gy)
    mean = jnp.mean(moments[:, 0], axis=0)
    shift = moments[:, 0] - mean
    variance = (jnp.sum(moments[:, 1], axis=0) + width * jnp.sum(shift * shift, axis=0)) / D
    inv_std = lax.rsqrt(variance + epsilon)
    x_hat = (x_float - mean[:, None]) * inv_std[:, None]
    normed = (x_hat * ln_gain + ln_bias).astype(bf16)

    upper = lax.axis_index("zh") == 1
    cotangent = jnp.concatenate(
        [
            jnp.where(upper, other_cotangent, grad_hidden),
            jnp.where(upper, grad_hidden, other_cotangent),
        ]
    ).astype(f32)

    partial_hidden = jnp.dot(normed, weight, preferred_element_type=f32).astype(bf16)
    arrived = exchange(partial_hidden.reshape(around, halves * rows, hidden_width), "x")
    half_sum = lax.reduce_precision(jnp.sum(arrived.astype(f32), axis=0), 8, 7)
    hidden = half_sum + swap(half_sum.astype(bf16)).astype(f32) + up_bias
    grad_pre = (cotangent * gelu_slope(hidden)).astype(bf16)
    grad_local = spread(grad_pre, "x").reshape(local, hidden_width)

    groups = lax.axis_size(gx)
    all_normed = lax.all_gather(normed, gx, axis=0, tiled=True)
    columns = exchange(
        grad_local.reshape(local, groups, hidden_width // groups).transpose(1, 0, 2), gx
    ).reshape(groups * local, hidden_width // groups)
    block_weight = lax.dot_general(
        all_normed, columns, (((0,), (0,)), ((), ())), preferred_element_type=f32
    ).astype(bf16)
    grad_weight = (
        exchange(block_weight.reshape(groups, sub_width, hidden_width // groups), gx)
        .transpose(1, 0, 2)
        .reshape(sub_width, hidden_width)
    )

    back = lax.dot_general(
        grad_local, weight, (((1,), (1,)), ((), ())), preferred_element_type=f32
    )
    sums = jnp.concatenate(
        [
            jnp.sum(back * x_hat, axis=0),
            jnp.sum(back, axis=0),
            jnp.sum(grad_local.astype(f32), axis=0),
        ]
    )
    sums = jnp.sum(spread(sums.reshape(-1, 128), gx), axis=0)
    norm_rows = 2 * width // 128
    grad_up_bias = sums[norm_rows:].reshape(hidden_width)
    norm_sums = jnp.sum(spread(sums[:norm_rows], "gz"), axis=0).reshape(2, width)
    grad_ln_gain, grad_ln_bias = norm_sums[0], norm_sums[1]
    landed = exchange(
        back.astype(bf16)
        .reshape(around, halves, rows, width)
        .transpose(1, 0, 2, 3)
        .reshape(depth, rows, width),
        "gz",
    )
    grad_float = jnp.sum(landed.astype(f32), axis=0).astype(bf16).astype(f32)

    def mine(value):
        ordered = value.reshape(around, halves, rows).transpose(1, 0, 2).reshape(depth, rows)
        return lax.dynamic_index_in_dim(ordered, lax.axis_index("gz"), 0, keepdims=False)[:, None]

    own_inv = mine(inv_std)
    own_hat = (inputs.astype(f32) - mine(mean)) * own_inv
    scaled = grad_float * ln_gain
    token_sums = jnp.stack([jnp.sum(scaled, axis=1), jnp.sum(scaled * own_hat, axis=1)])
    first_total, second_total = jnp.sum(spread(token_sums, gy), axis=0)
    grad_inputs = (
        own_inv * (scaled - first_total[:, None] / D - own_hat * (second_total[:, None] / D))
    ).astype(bf16)
    return (grad_inputs, grad_weight, grad_up_bias, grad_ln_gain, grad_ln_bias)


def solution(mesh):
    cube = Mesh(mesh.devices.reshape(4, 2, 2, 4, 8), ("y", "core", "zh", "x", "gz"))
    return jax.shard_map(
        shards,
        mesh=cube,
        in_specs=(
            P(("y", "core", "gz"), gy),
            P(gy),
            P(gy),
            P(("zh", "x", "y", "core"), "gz"),
            P("gz"),
            P(("y", "core", "zh", "x"), "gz"),
        ),
        out_specs=(
            P(("y", "core", "gz"), gy),
            P(("zh", "x", "y", "core"), "gz"),
            P("gz"),
            P(gy),
            P(gy),
        ),
        check_vma=False,
    )
```

```python
import math

import jax
import jax.numpy as jnp
from jax import lax
from jax.sharding import Mesh, PartitionSpec as P

D = 12288


gelu_scale = math.sqrt(2.0 / math.pi)
cubic = 0.044715
epsilon = 1e-05

gx = ("y", "core")
gy = ("zh", "x")


def gelu_slope(value):
    inner = gelu_scale * (value + cubic * value * value * value)
    tangent = jnp.tanh(inner)
    return 0.5 * (1.0 + tangent) + 0.5 * value * (1.0 - tangent * tangent) * gelu_scale * (
        1.0 + 3.0 * cubic * value * value
    )


def exchange(blocks, axis):
    return lax.all_to_all(blocks, axis, split_axis=0, concat_axis=0, tiled=True)


def spread(block, axis):
    count = lax.axis_size(axis)
    return exchange(jnp.broadcast_to(block[None], (count,) + block.shape), axis)


def swap(block):
    return lax.ppermute(block, "zh", [(0, 1), (1, 0)])


def shards(inputs, ln_gain, ln_bias, weight_in, up_bias, grad_hidden):
    f32, bf16 = jnp.float32, jnp.bfloat16
    rows, width = inputs.shape
    hidden_width = weight_in.shape[1]
    sub_width = weight_in.shape[0]
    depth = lax.axis_size("gz")
    halves, around = lax.axis_size("zh"), lax.axis_size("x")
    local = depth * rows

    weight = lax.all_gather(weight_in, gx, axis=0, tiled=True)

    x_float = (
        spread(inputs, "gz")
        .reshape(halves, around, rows, width)
        .transpose(1, 0, 2, 3)
        .reshape(local, width)
        .astype(f32)
    )
    own_mean = jnp.mean(x_float, axis=1)
    own_centered = x_float - own_mean[:, None]
    own_square = jnp.sum(own_centered * own_centered, axis=1)
    other_cotangent = swap(grad_hidden)
    own_square = own_square + 0.0 * other_cotangent[0, 0].astype(f32)
    moments = spread(jnp.stack([own_mean, own_square]), gy)
    mean = jnp.mean(moments[:, 0], axis=0)
    shift = moments[:, 0] - mean
    variance = (jnp.sum(moments[:, 1], axis=0) + width * jnp.sum(shift * shift, axis=0)) / D
    inv_std = lax.rsqrt(variance + epsilon)
    x_hat = (x_float - mean[:, None]) * inv_std[:, None]
    normed = (x_hat * ln_gain + ln_bias).astype(bf16)

    upper = lax.axis_index("zh") == 1
    cotangent = jnp.concatenate(
        [
            jnp.where(upper, other_cotangent, grad_hidden),
            jnp.where(upper, grad_hidden, other_cotangent),
        ]
    ).astype(f32)

    partial_hidden = jnp.dot(normed, weight, preferred_element_type=f32).astype(bf16)
    arrived = exchange(partial_hidden.reshape(around, halves * rows, hidden_width), "x")
    half_sum = lax.reduce_precision(jnp.sum(arrived.astype(f32), axis=0), 8, 7)
    hidden = half_sum + swap(half_sum.astype(bf16)).astype(f32) + up_bias
    grad_pre = (cotangent * gelu_slope(hidden)).astype(bf16)
    grad_local = spread(grad_pre, "x").reshape(local, hidden_width)

    all_normed = lax.all_gather(normed, gx, axis=0, tiled=True)
    portion = lax.all_gather(grad_local, gx, axis=0, tiled=True)

    back = lax.dot_general(
        grad_local, weight, (((1,), (1,)), ((), ())), preferred_element_type=f32
    )
    sums = jnp.stack([jnp.sum(back * x_hat, axis=0), jnp.sum(back, axis=0)]).astype(bf16)
    packed = 2 * width // rows
    padding = -packed % 128
    extra = jnp.pad(sums.reshape(rows, packed), ((0, 0), (0, padding)))
    ordered = (
        back.astype(bf16)
        .reshape(around, halves, rows, width)
        .transpose(1, 0, 2, 3)
        .reshape(depth, rows, width)
    )
    landed = exchange(
        jnp.concatenate([ordered, jnp.broadcast_to(extra[None], (depth,) + extra.shape)], axis=2),
        "gz",
    )
    total = jnp.sum(landed.astype(f32), axis=0)
    grad_float = total[:, :width].astype(bf16).astype(f32)
    small = jnp.concatenate(
        [
            total[:, width : width + packed].reshape(2 * width),
            jnp.sum(grad_local.astype(f32), axis=0),
        ]
    ).reshape(-1, 128)
    small = small + lax.ppermute(small, "core", [(0, 1), (1, 0)])
    small = small + lax.ppermute(small, "y", [(0, 1), (1, 0), (2, 3), (3, 2)])
    small = small + lax.ppermute(small, "y", [(0, 3), (3, 0), (1, 2), (2, 1)])
    small = small.reshape(-1)
    grad_ln_gain, grad_ln_bias = small[:width], small[width : 2 * width]
    grad_up_bias = small[2 * width :]

    def mine(value):
        ordered = value.reshape(around, halves, rows).transpose(1, 0, 2).reshape(depth, rows)
        return lax.dynamic_index_in_dim(ordered, lax.axis_index("gz"), 0, keepdims=False)[:, None]

    own_inv = mine(inv_std)
    own_hat = (inputs.astype(f32) - mine(mean)) * own_inv
    scaled = grad_float * ln_gain
    token_sums = jnp.stack([jnp.sum(scaled, axis=1), jnp.sum(scaled * own_hat, axis=1)])
    first_total, second_total = jnp.sum(spread(token_sums, gy), axis=0)
    grad_inputs = (
        own_inv * (scaled - first_total[:, None] / D - own_hat * (second_total[:, None] / D))
    ).astype(bf16)
    feature_rows = lax.dynamic_slice_in_dim(
        all_normed, lax.axis_index(gx) * sub_width, sub_width, axis=1
    )
    grad_weight = lax.dot_general(
        feature_rows, portion, (((0,), (0,)), ((), ())), preferred_element_type=f32
    ).astype(bf16)
    return (grad_inputs, grad_weight, grad_up_bias, grad_ln_gain, grad_ln_bias)


def solution(mesh):
    cube = Mesh(mesh.devices.reshape(4, 2, 2, 4, 8), ("y", "core", "zh", "x", "gz"))
    return jax.shard_map(
        shards,
        mesh=cube,
        in_specs=(
            P(("y", "core", "gz"), gy),
            P(gy),
            P(gy),
            P(("zh", "x", "y", "core"), "gz"),
            P("gz"),
            P(("y", "core", "zh", "x"), "gz"),
        ),
        out_specs=(
            P(("y", "core", "gz"), gy),
            P(("zh", "x", "y", "core"), "gz"),
            P("gz"),
            P(gy),
            P(gy),
        ),
        check_vma=False,
    )
```

```python
import math

import jax
import jax.numpy as jnp
from jax import lax
from jax.sharding import Mesh, PartitionSpec as P

D = 12288


gelu_scale = math.sqrt(2.0 / math.pi)
cubic = 0.044715
epsilon = 1e-05

gx = ("y", "core")
gy = ("zh", "x")


def gelu_slope(value):
    inner = gelu_scale * (value + cubic * value * value * value)
    tangent = jnp.tanh(inner)
    return 0.5 * (1.0 + tangent) + 0.5 * value * (1.0 - tangent * tangent) * gelu_scale * (
        1.0 + 3.0 * cubic * value * value
    )


def exchange(blocks, axis):
    return lax.all_to_all(blocks, axis, split_axis=0, concat_axis=0, tiled=True)


def spread(block, axis):
    count = lax.axis_size(axis)
    return exchange(jnp.broadcast_to(block[None], (count,) + block.shape), axis)


def swap(block):
    return lax.ppermute(block, "zh", [(0, 1), (1, 0)])


def split_float(value):
    high = lax.reduce_precision(value, 8, 7)
    return high, value - high


def shards(inputs, ln_gain, ln_bias, weight_in, up_bias, grad_hidden):
    f32, bf16 = jnp.float32, jnp.bfloat16
    rows, width = inputs.shape
    hidden_width = weight_in.shape[1]
    sub_width = weight_in.shape[0]
    depth = lax.axis_size("gz")
    halves, around = lax.axis_size("zh"), lax.axis_size("x")
    local = depth * rows

    weight = lax.all_gather(weight_in, gx, axis=0, tiled=True)

    x_float = (
        spread(inputs, "gz")
        .reshape(halves, around, rows, width)
        .transpose(1, 0, 2, 3)
        .reshape(local, width)
        .astype(f32)
    )
    own_mean = jnp.mean(x_float, axis=1)
    own_centered = x_float - own_mean[:, None]
    own_square = jnp.sum(own_centered * own_centered, axis=1)
    other_cotangent = swap(grad_hidden)
    own_square = own_square + 0.0 * other_cotangent[0, 0].astype(f32)
    moments = spread(jnp.stack([own_mean, own_square]), gy)
    mean = jnp.mean(moments[:, 0], axis=0)
    shift = moments[:, 0] - mean
    variance = (jnp.sum(moments[:, 1], axis=0) + width * jnp.sum(shift * shift, axis=0)) / D
    inv_std = lax.rsqrt(variance + epsilon)
    x_hat = (x_float - mean[:, None]) * inv_std[:, None]
    normed = (x_hat * ln_gain + ln_bias).astype(bf16)

    upper = lax.axis_index("zh") == 1
    cotangent = jnp.concatenate(
        [
            jnp.where(upper, other_cotangent, grad_hidden),
            jnp.where(upper, grad_hidden, other_cotangent),
        ]
    ).astype(f32)

    extra_rows = 8
    block = halves * rows
    affine = jnp.stack([*split_float(ln_gain), *split_float(ln_bias)]).astype(bf16)
    affine = jnp.pad(affine, ((0, extra_rows - 4), (0, 0)))
    stacked = jnp.concatenate(
        [
            normed.reshape(around, block, width),
            jnp.broadcast_to(affine[None], (around,) + affine.shape),
        ],
        axis=1,
    )
    partial_hidden = jnp.dot(
        stacked.reshape(-1, width), weight, preferred_element_type=f32
    ).astype(bf16)
    arrived = exchange(partial_hidden.reshape(around, block + extra_rows, hidden_width), "x")
    half_sum = lax.reduce_precision(jnp.sum(arrived.astype(f32), axis=0), 8, 7)
    products = half_sum + swap(half_sum.astype(bf16)).astype(f32)
    product = products[:block]
    gain_product = products[block] + products[block + 1]
    bias_product = products[block + 2] + products[block + 3]
    grad_pre = (cotangent * gelu_slope(product + up_bias)).astype(bf16)
    grad_pre_float = grad_pre.astype(f32)
    token_sums = jnp.stack(
        [
            jnp.sum(grad_pre_float * gain_product, axis=1),
            jnp.sum(grad_pre_float * (product - bias_product), axis=1),
        ]
    )
    token_rows = jnp.concatenate(split_float(token_sums)).astype(bf16)
    token_rows = jnp.pad(token_rows, ((0, extra_rows - 4), (0, hidden_width - block)))
    around_rows = spread(jnp.concatenate([grad_pre, token_rows]), "x")
    grad_local = around_rows[:, :block].reshape(local, hidden_width)
    token_parts = (
        around_rows[:, block : block + 4, :block]
        .reshape(around, 4, halves, rows)
        .transpose(2, 0, 3, 1)
        .reshape(depth, rows, 4)
    )

    all_normed = lax.all_gather(normed, gx, axis=0, tiled=True)
    portion = lax.all_gather(grad_local, gx, axis=0, tiled=True)

    back = lax.dot_general(
        grad_local, weight, (((1,), (1,)), ((), ())), preferred_element_type=f32
    )
    sums = jnp.stack([jnp.sum(back * x_hat, axis=0), jnp.sum(back, axis=0)]).astype(bf16)
    packed = 2 * width // rows
    padding = -(packed + 4) % 128
    ordered = (
        back.astype(bf16)
        .reshape(around, halves, rows, width)
        .transpose(1, 0, 2, 3)
        .reshape(depth, rows, width)
    )
    landed = exchange(
        jnp.concatenate(
            [
                ordered,
                jnp.broadcast_to(sums.reshape(1, rows, packed), (depth, rows, packed)),
                token_parts,
                jnp.zeros((depth, rows, padding), bf16),
            ],
            axis=2,
        ),
        "gz",
    )
    total = jnp.sum(landed.astype(f32), axis=0)
    grad_float = total[:, :width].astype(bf16).astype(f32)
    small = jnp.concatenate(
        [
            total[:, width : width + packed].reshape(2 * width),
            jnp.sum(grad_local.astype(f32), axis=0),
        ]
    ).reshape(-1, 128)
    small = jnp.sum(spread(small, gx), axis=0).reshape(-1)
    grad_ln_gain, grad_ln_bias = small[:width], small[width : 2 * width]
    grad_up_bias = small[2 * width :]

    def mine(value):
        ordered = value.reshape(around, halves, rows).transpose(1, 0, 2).reshape(depth, rows)
        return lax.dynamic_index_in_dim(ordered, lax.axis_index("gz"), 0, keepdims=False)[:, None]

    own_inv = mine(inv_std)
    own_hat = (inputs.astype(f32) - mine(mean)) * own_inv
    scaled = grad_float * ln_gain
    parts = total[:, width + packed : width + packed + 4]
    first_total = parts[:, 0] + parts[:, 2]
    second_total = parts[:, 1] + parts[:, 3]
    grad_inputs = (
        own_inv * (scaled - first_total[:, None] / D - own_hat * (second_total[:, None] / D))
    ).astype(bf16)
    feature_rows = lax.dynamic_slice_in_dim(
        all_normed, lax.axis_index(gx) * sub_width, sub_width, axis=1
    )
    grad_weight = lax.dot_general(
        feature_rows, portion, (((0,), (0,)), ((), ())), preferred_element_type=f32
    ).astype(bf16)
    return (grad_inputs, grad_weight, grad_up_bias, grad_ln_gain, grad_ln_bias)


def solution(mesh):
    cube = Mesh(mesh.devices.reshape(4, 2, 2, 4, 8), ("y", "core", "zh", "x", "gz"))
    return jax.shard_map(
        shards,
        mesh=cube,
        in_specs=(
            P(("y", "core", "gz"), gy),
            P(gy),
            P(gy),
            P(("zh", "x", "y", "core"), "gz"),
            P("gz"),
            P(("y", "core", "zh", "x"), "gz"),
        ),
        out_specs=(
            P(("y", "core", "gz"), gy),
            P(("zh", "x", "y", "core"), "gz"),
            P("gz"),
            P(gy),
            P(gy),
        ),
        check_vma=False,
    )
```

```python
import math

import jax
import jax.numpy as jnp
from jax import lax
from jax.sharding import Mesh, PartitionSpec as P

D = 12288


gelu_scale = math.sqrt(2.0 / math.pi)
cubic = 0.044715
epsilon = 1e-05

gx = ("y", "core")
gy = ("zh", "x")


def gelu_slope(value):
    inner = gelu_scale * (value + cubic * value * value * value)
    tangent = jnp.tanh(inner)
    return 0.5 * (1.0 + tangent) + 0.5 * value * (1.0 - tangent * tangent) * gelu_scale * (
        1.0 + 3.0 * cubic * value * value
    )


def exchange(blocks, axis):
    return lax.all_to_all(blocks, axis, split_axis=0, concat_axis=0, tiled=True)


def spread(block, axis):
    count = lax.axis_size(axis)
    return exchange(jnp.broadcast_to(block[None], (count,) + block.shape), axis)


def swap(block):
    return lax.ppermute(block, "zh", [(0, 1), (1, 0)])


def split_float(value):
    high = lax.reduce_precision(value, 8, 7)
    return high, value - high


def shards(inputs, ln_gain, ln_bias, weight_in, up_bias, grad_hidden):
    f32, bf16 = jnp.float32, jnp.bfloat16
    rows, width = inputs.shape
    hidden_width = weight_in.shape[1]
    sub_width = weight_in.shape[0]
    depth = lax.axis_size("gz")
    halves, around = lax.axis_size("zh"), lax.axis_size("x")
    local = depth * rows

    weight = lax.all_gather(weight_in, gx, axis=0, tiled=True)

    x_float = (
        spread(inputs, "gz")
        .reshape(halves, around, rows, width)
        .transpose(1, 0, 2, 3)
        .reshape(local, width)
        .astype(f32)
    )
    own_mean = jnp.mean(x_float, axis=1)
    own_centered = x_float - own_mean[:, None]
    own_square = jnp.sum(own_centered * own_centered, axis=1)
    other_cotangent = swap(grad_hidden)
    own_square = own_square + 0.0 * other_cotangent[0, 0].astype(f32)
    moments = spread(jnp.stack([own_mean, own_square]), gy)
    mean = jnp.mean(moments[:, 0], axis=0)
    shift = moments[:, 0] - mean
    variance = (jnp.sum(moments[:, 1], axis=0) + width * jnp.sum(shift * shift, axis=0)) / D
    inv_std = lax.rsqrt(variance + epsilon)
    x_hat = (x_float - mean[:, None]) * inv_std[:, None]
    normed = (x_hat * ln_gain + ln_bias).astype(bf16)

    upper = lax.axis_index("zh") == 1
    cotangent = jnp.concatenate(
        [
            jnp.where(upper, other_cotangent, grad_hidden),
            jnp.where(upper, grad_hidden, other_cotangent),
        ]
    ).astype(f32)

    extra_rows = 8
    block = halves * rows
    affine = jnp.stack([*split_float(ln_gain), *split_float(ln_bias)]).astype(bf16)
    affine = jnp.pad(affine, ((0, extra_rows - 4), (0, 0)))
    stacked = jnp.concatenate(
        [
            normed.reshape(around, block, width),
            jnp.broadcast_to(affine[None], (around,) + affine.shape),
        ],
        axis=1,
    )
    stacked = stacked.reshape(-1, width)
    all_stacked = lax.all_gather(stacked, gx, axis=0, tiled=True)
    partial_hidden = jnp.dot(stacked, weight, preferred_element_type=f32).astype(bf16)
    arrived = exchange(partial_hidden.reshape(around, block + extra_rows, hidden_width), "x")
    half_sum = lax.reduce_precision(jnp.sum(arrived.astype(f32), axis=0), 8, 7)
    products = half_sum + swap(half_sum.astype(bf16)).astype(f32)
    product = products[:block]
    gain_product = products[block] + products[block + 1]
    bias_product = products[block + 2] + products[block + 3]
    grad_pre = (cotangent * gelu_slope(product + up_bias)).astype(bf16)
    grad_pre_float = grad_pre.astype(f32)
    token_sums = jnp.stack(
        [
            jnp.sum(grad_pre_float * gain_product, axis=1),
            jnp.sum(grad_pre_float * (product - bias_product), axis=1),
        ]
    )
    token_rows = jnp.concatenate(split_float(token_sums)).astype(bf16)
    token_rows = jnp.pad(token_rows, ((0, extra_rows - 4), (0, hidden_width - block)))
    around_rows = spread(jnp.concatenate([grad_pre, token_rows]), "x")
    grad_local = around_rows[:, :block].reshape(local, hidden_width)
    token_parts = (
        around_rows[:, block : block + 4, :block]
        .reshape(around, 4, halves, rows)
        .transpose(2, 0, 3, 1)
        .reshape(depth, rows, 4)
    )

    portion = lax.all_gather(grad_local, gx, axis=0, tiled=True)

    back = lax.dot_general(
        grad_local, weight, (((1,), (1,)), ((), ())), preferred_element_type=f32
    )
    sums = jnp.stack([jnp.sum(back * x_hat, axis=0), jnp.sum(back, axis=0)]).astype(bf16)
    packed = 2 * width // rows
    padding = -(packed + 4) % 128
    ordered = (
        back.astype(bf16)
        .reshape(around, halves, rows, width)
        .transpose(1, 0, 2, 3)
        .reshape(depth, rows, width)
    )
    landed = exchange(
        jnp.concatenate(
            [
                ordered,
                jnp.broadcast_to(sums.reshape(1, rows, packed), (depth, rows, packed)),
                token_parts,
                jnp.zeros((depth, rows, padding), bf16),
            ],
            axis=2,
        ),
        "gz",
    )
    total = jnp.sum(landed.astype(f32), axis=0)
    grad_float = total[:, :width].astype(bf16).astype(f32)
    small = jnp.concatenate(
        [
            total[:, width : width + packed].reshape(2 * width),
            jnp.sum(grad_local.astype(f32), axis=0),
        ]
    ).reshape(-1, 128)
    small = jnp.sum(spread(small, gx), axis=0).reshape(-1)
    grad_ln_gain, grad_ln_bias = small[:width], small[width : 2 * width]
    grad_up_bias = small[2 * width :]

    def mine(value):
        ordered = value.reshape(around, halves, rows).transpose(1, 0, 2).reshape(depth, rows)
        return lax.dynamic_index_in_dim(ordered, lax.axis_index("gz"), 0, keepdims=False)[:, None]

    own_inv = mine(inv_std)
    own_hat = (inputs.astype(f32) - mine(mean)) * own_inv
    scaled = grad_float * ln_gain
    parts = total[:, width + packed : width + packed + 4]
    first_total = parts[:, 0] + parts[:, 2]
    second_total = parts[:, 1] + parts[:, 3]
    grad_inputs = (
        own_inv * (scaled - first_total[:, None] / D - own_hat * (second_total[:, None] / D))
    ).astype(bf16)
    feature_rows = (
        lax.dynamic_slice_in_dim(all_stacked, lax.axis_index(gx) * sub_width, sub_width, axis=1)
        .reshape(-1, block + extra_rows, sub_width)[:, :block]
        .reshape(-1, sub_width)
    )
    grad_weight = lax.dot_general(
        feature_rows, portion, (((0,), (0,)), ((), ())), preferred_element_type=f32
    ).astype(bf16)
    return (grad_inputs, grad_weight, grad_up_bias, grad_ln_gain, grad_ln_bias)


def solution(mesh):
    cube = Mesh(mesh.devices.reshape(4, 2, 2, 4, 8), ("y", "core", "zh", "x", "gz"))
    return jax.shard_map(
        shards,
        mesh=cube,
        in_specs=(
            P(("y", "core", "gz"), gy),
            P(gy),
            P(gy),
            P(("zh", "x", "y", "core"), "gz"),
            P("gz"),
            P(("y", "core", "zh", "x"), "gz"),
        ),
        out_specs=(
            P(("y", "core", "gz"), gy),
            P(("zh", "x", "y", "core"), "gz"),
            P("gz"),
            P(gy),
            P(gy),
        ),
        check_vma=False,
    )
```

```python
import math

import jax
import jax.numpy as jnp
from jax import lax
from jax.sharding import Mesh, PartitionSpec as P

D = 12288


gelu_scale = math.sqrt(2.0 / math.pi)
cubic = 0.044715
epsilon = 1e-05

gx = ("y", "core")
gy = ("zh", "x")


def gelu_slope(value):
    inner = gelu_scale * (value + cubic * value * value * value)
    tangent = jnp.tanh(inner)
    return 0.5 * (1.0 + tangent) + 0.5 * value * (1.0 - tangent * tangent) * gelu_scale * (
        1.0 + 3.0 * cubic * value * value
    )


def exchange(blocks, axis):
    return lax.all_to_all(blocks, axis, split_axis=0, concat_axis=0, tiled=True)


def spread(block, axis):
    count = lax.axis_size(axis)
    return exchange(jnp.broadcast_to(block[None], (count,) + block.shape), axis)


def swap(block):
    return lax.ppermute(block, "zh", [(0, 1), (1, 0)])


def split_float(value):
    high = lax.reduce_precision(value, 8, 7)
    return high, value - high


def shards(inputs, ln_gain, ln_bias, weight_in, up_bias, grad_hidden):
    f32, bf16 = jnp.float32, jnp.bfloat16
    rows, width = inputs.shape
    hidden_width = weight_in.shape[1]
    sub_width = weight_in.shape[0]
    depth = lax.axis_size("gz")
    halves, around = lax.axis_size("zh"), lax.axis_size("x")
    local = depth * rows

    weight = lax.all_gather(weight_in, gx, axis=0, tiled=True)

    x_float = (
        spread(inputs, "gz")
        .reshape(halves, around, rows, width)
        .transpose(1, 0, 2, 3)
        .reshape(local, width)
        .astype(f32)
    )
    own_mean = jnp.mean(x_float, axis=1)
    own_centered = x_float - own_mean[:, None]
    own_square = jnp.sum(own_centered * own_centered, axis=1)
    other_cotangent = swap(grad_hidden)
    own_square = own_square + 0.0 * other_cotangent[0, 0].astype(f32)
    moments = spread(jnp.stack([own_mean, own_square]), gy)
    mean = jnp.mean(moments[:, 0], axis=0)
    shift = moments[:, 0] - mean
    variance = (jnp.sum(moments[:, 1], axis=0) + width * jnp.sum(shift * shift, axis=0)) / D
    inv_std = lax.rsqrt(variance + epsilon)
    x_hat = (x_float - mean[:, None]) * inv_std[:, None]
    normed = (x_hat * ln_gain + ln_bias).astype(bf16)

    upper = lax.axis_index("zh") == 1
    cotangent = jnp.concatenate(
        [
            jnp.where(upper, other_cotangent, grad_hidden),
            jnp.where(upper, grad_hidden, other_cotangent),
        ]
    ).astype(f32)

    extra_rows = 8
    block = halves * rows
    affine = jnp.stack([*split_float(ln_gain), *split_float(ln_bias)]).astype(bf16)
    affine = jnp.pad(affine, ((0, extra_rows - 4), (0, 0)))
    stacked = jnp.concatenate(
        [
            normed.reshape(around, block, width),
            jnp.broadcast_to(affine[None], (around,) + affine.shape),
        ],
        axis=1,
    )
    stacked = stacked.reshape(-1, width)
    all_stacked = lax.all_gather(stacked, gx, axis=0, tiled=True)
    pieces = 2
    piece = hidden_width // pieces
    local_parts, sums_parts = [], []
    for index in range(pieces):
        span = slice(index * piece, (index + 1) * piece)
        partial_hidden = jnp.dot(stacked, weight[:, span], preferred_element_type=f32).astype(bf16)
        arrived = exchange(partial_hidden.reshape(around, block + extra_rows, piece), "x")
        half_sum = lax.reduce_precision(jnp.sum(arrived.astype(f32), axis=0), 8, 7)
        products = half_sum + swap(half_sum.astype(bf16)).astype(f32)
        if index:
            products = products + 0.0 * local_parts[-1][0, 0].astype(f32)
        product = products[:block]
        gain_product = products[block] + products[block + 1]
        bias_product = products[block + 2] + products[block + 3]
        grad_pre = (cotangent[:, span] * gelu_slope(product + up_bias[span])).astype(bf16)
        grad_pre_float = grad_pre.astype(f32)
        sums_parts.append(
            jnp.stack(
                [
                    jnp.sum(grad_pre_float * gain_product, axis=1),
                    jnp.sum(grad_pre_float * (product - bias_product), axis=1),
                ]
            )
        )
        if index == pieces - 1:
            token_rows = jnp.concatenate(split_float(sum(sums_parts))).astype(bf16)
            token_rows = jnp.pad(token_rows, ((0, extra_rows - 4), (0, piece - block)))
            grad_pre = jnp.concatenate([grad_pre, token_rows])
        around_rows = spread(grad_pre, "x")
        local_parts.append(around_rows[:, :block].reshape(local, piece))
    grad_local = jnp.concatenate(local_parts, axis=1)
    token_parts = (
        around_rows[:, block : block + 4, :block]
        .reshape(around, 4, halves, rows)
        .transpose(2, 0, 3, 1)
        .reshape(depth, rows, 4)
    )

    portion = lax.all_gather(grad_local, gx, axis=0, tiled=True)

    back = lax.dot_general(
        grad_local, weight, (((1,), (1,)), ((), ())), preferred_element_type=f32
    )
    sums = jnp.stack([jnp.sum(back * x_hat, axis=0), jnp.sum(back, axis=0)]).astype(bf16)
    packed = 2 * width // rows
    padding = -(packed + 4) % 128
    ordered = (
        back.astype(bf16)
        .reshape(around, halves, rows, width)
        .transpose(1, 0, 2, 3)
        .reshape(depth, rows, width)
    )
    landed = exchange(
        jnp.concatenate(
            [
                ordered,
                jnp.broadcast_to(sums.reshape(1, rows, packed), (depth, rows, packed)),
                token_parts,
                jnp.zeros((depth, rows, padding), bf16),
            ],
            axis=2,
        ),
        "gz",
    )
    total = jnp.sum(landed.astype(f32), axis=0)
    grad_float = total[:, :width].astype(bf16).astype(f32)
    small = jnp.concatenate(
        [
            total[:, width : width + packed].reshape(2 * width),
            jnp.sum(grad_local.astype(f32), axis=0),
        ]
    ).reshape(-1, 128)
    small = jnp.sum(spread(small, gx), axis=0).reshape(-1)
    grad_ln_gain, grad_ln_bias = small[:width], small[width : 2 * width]
    grad_up_bias = small[2 * width :]

    def mine(value):
        ordered = value.reshape(around, halves, rows).transpose(1, 0, 2).reshape(depth, rows)
        return lax.dynamic_index_in_dim(ordered, lax.axis_index("gz"), 0, keepdims=False)[:, None]

    own_inv = mine(inv_std)
    own_hat = (inputs.astype(f32) - mine(mean)) * own_inv
    scaled = grad_float * ln_gain
    parts = total[:, width + packed : width + packed + 4]
    first_total = parts[:, 0] + parts[:, 2]
    second_total = parts[:, 1] + parts[:, 3]
    grad_inputs = (
        own_inv * (scaled - first_total[:, None] / D - own_hat * (second_total[:, None] / D))
    ).astype(bf16)
    feature_rows = (
        lax.dynamic_slice_in_dim(all_stacked, lax.axis_index(gx) * sub_width, sub_width, axis=1)
        .reshape(-1, block + extra_rows, sub_width)[:, :block]
        .reshape(-1, sub_width)
    )
    grad_weight = lax.dot_general(
        feature_rows, portion, (((0,), (0,)), ((), ())), preferred_element_type=f32
    ).astype(bf16)
    grad_up_bias = grad_up_bias + 0.0 * grad_weight[0, 0].astype(f32)
    return (grad_inputs, grad_weight, grad_up_bias, grad_ln_gain, grad_ln_bias)


def solution(mesh):
    cube = Mesh(mesh.devices.reshape(4, 2, 2, 4, 8), ("y", "core", "zh", "x", "gz"))
    return jax.shard_map(
        shards,
        mesh=cube,
        in_specs=(
            P(("y", "core", "gz"), gy),
            P(gy),
            P(gy),
            P(("zh", "x", "y", "core"), "gz"),
            P("gz"),
            P(("y", "core", "zh", "x"), "gz"),
        ),
        out_specs=(
            P(("y", "core", "gz"), gy),
            P(("zh", "x", "y", "core"), "gz"),
            P("gz"),
            P(gy),
            P(gy),
        ),
        check_vma=False,
    )
```

```python
import math

import jax
import jax.numpy as jnp
from jax import lax
from jax.sharding import Mesh, PartitionSpec as P

D = 12288


gelu_scale = math.sqrt(2.0 / math.pi)
cubic = 0.044715
epsilon = 1e-05

gx = ("y", "core")
gy = ("zh", "x")


def gelu_slope(value):
    inner = gelu_scale * (value + cubic * value * value * value)
    tangent = jnp.tanh(inner)
    return 0.5 * (1.0 + tangent) + 0.5 * value * (1.0 - tangent * tangent) * gelu_scale * (
        1.0 + 3.0 * cubic * value * value
    )


def exchange(blocks, axis):
    return lax.all_to_all(blocks, axis, split_axis=0, concat_axis=0, tiled=True)


def spread(block, axis):
    count = lax.axis_size(axis)
    return exchange(jnp.broadcast_to(block[None], (count,) + block.shape), axis)


def swap(block):
    return lax.ppermute(block, "zh", [(0, 1), (1, 0)])


def split_float(value):
    high = lax.reduce_precision(value, 8, 7)
    return high, value - high


def shards(inputs, ln_gain, ln_bias, weight_in, up_bias, grad_hidden):
    f32, bf16 = jnp.float32, jnp.bfloat16
    rows, width = inputs.shape
    hidden_width = weight_in.shape[1]
    sub_width = weight_in.shape[0]
    depth = lax.axis_size("gz")
    halves, around = lax.axis_size("zh"), lax.axis_size("x")
    local = depth * rows

    weight = lax.all_gather(weight_in, gx, axis=0, tiled=True)

    x_float = (
        spread(inputs, "gz")
        .reshape(halves, around, rows, width)
        .transpose(1, 0, 2, 3)
        .reshape(local, width)
        .astype(f32)
    )
    own_mean = jnp.mean(x_float, axis=1)
    own_centered = x_float - own_mean[:, None]
    own_square = jnp.sum(own_centered * own_centered, axis=1)
    other_cotangent = swap(grad_hidden)
    own_square = own_square + 0.0 * other_cotangent[0, 0].astype(f32)
    moments = spread(jnp.stack([own_mean, own_square]), gy)
    mean = jnp.mean(moments[:, 0], axis=0)
    shift = moments[:, 0] - mean
    variance = (jnp.sum(moments[:, 1], axis=0) + width * jnp.sum(shift * shift, axis=0)) / D
    inv_std = lax.rsqrt(variance + epsilon)
    x_hat = (x_float - mean[:, None]) * inv_std[:, None]
    normed = (x_hat * ln_gain + ln_bias).astype(bf16)

    upper = lax.axis_index("zh") == 1
    cotangent = jnp.concatenate(
        [
            jnp.where(upper, other_cotangent, grad_hidden),
            jnp.where(upper, grad_hidden, other_cotangent),
        ]
    ).astype(f32)

    extra_rows = 8
    block = halves * rows
    affine = jnp.stack([*split_float(ln_gain), *split_float(ln_bias)]).astype(bf16)
    stacked = jnp.concatenate([normed, jnp.pad(affine, ((0, extra_rows - 4), (0, 0)))])
    all_stacked = lax.all_gather(stacked, gx, axis=0, tiled=True)
    partial_hidden = jnp.dot(stacked, weight, preferred_element_type=f32).astype(bf16)
    affine_parts = partial_hidden[local : local + 4].astype(f32)
    affine_parts = (affine_parts[0::2] + affine_parts[1::2]).astype(bf16)
    share = 2 * hidden_width // block
    affine_parts = jnp.pad(affine_parts.reshape(block, share), ((0, 0), (0, -share % 128)))
    arrived = exchange(
        jnp.concatenate(
            [
                partial_hidden[:local].reshape(around, block, hidden_width),
                jnp.broadcast_to(affine_parts[None], (around,) + affine_parts.shape),
            ],
            axis=2,
        ),
        "x",
    )
    half_sum = lax.reduce_precision(jnp.sum(arrived.astype(f32), axis=0), 8, 7)
    products = half_sum + swap(half_sum.astype(bf16)).astype(f32)
    product = products[:, :hidden_width]
    affine_product = products[:, hidden_width : hidden_width + share].reshape(2, hidden_width)
    grad_pre = (cotangent * gelu_slope(product + up_bias)).astype(bf16)
    grad_pre_float = grad_pre.astype(f32)
    token_sums = jnp.stack(
        [
            jnp.sum(grad_pre_float * affine_product[0], axis=1),
            jnp.sum(grad_pre_float * (product - affine_product[1]), axis=1),
        ],
        axis=1,
    )
    token_columns = jnp.concatenate(split_float(token_sums), axis=1).astype(bf16)
    around_rows = spread(
        jnp.concatenate([grad_pre, jnp.pad(token_columns, ((0, 0), (0, 124)))], axis=1), "x"
    )
    grad_local = around_rows[:, :, :hidden_width].reshape(local, hidden_width)
    token_parts = (
        around_rows[:, :, hidden_width : hidden_width + 4]
        .reshape(around, halves, rows, 4)
        .transpose(1, 0, 2, 3)
        .reshape(depth, rows, 4)
    )

    portion = lax.all_gather(grad_local, gx, axis=0, tiled=True)

    back = lax.dot_general(
        grad_local, weight, (((1,), (1,)), ((), ())), preferred_element_type=f32
    )
    sums = jnp.stack([jnp.sum(back * x_hat, axis=0), jnp.sum(back, axis=0)]).astype(bf16)
    packed = 2 * width // rows
    padding = -(packed + 4) % 128
    ordered = (
        back.astype(bf16)
        .reshape(around, halves, rows, width)
        .transpose(1, 0, 2, 3)
        .reshape(depth, rows, width)
    )
    landed = exchange(
        jnp.concatenate(
            [
                ordered,
                jnp.broadcast_to(sums.reshape(1, rows, packed), (depth, rows, packed)),
                token_parts,
                jnp.zeros((depth, rows, padding), bf16),
            ],
            axis=2,
        ),
        "gz",
    )
    total = jnp.sum(landed.astype(f32), axis=0)
    grad_float = total[:, :width].astype(bf16).astype(f32)
    small = jnp.concatenate(
        [
            total[:, width : width + packed].reshape(2 * width),
            jnp.sum(grad_local.astype(f32), axis=0),
        ]
    ).reshape(-1, 128)
    small = jnp.sum(spread(small, gx), axis=0).reshape(-1)
    grad_ln_gain, grad_ln_bias = small[:width], small[width : 2 * width]
    grad_up_bias = small[2 * width :]

    def mine(value):
        ordered = value.reshape(around, halves, rows).transpose(1, 0, 2).reshape(depth, rows)
        return lax.dynamic_index_in_dim(ordered, lax.axis_index("gz"), 0, keepdims=False)[:, None]

    own_inv = mine(inv_std)
    own_hat = (inputs.astype(f32) - mine(mean)) * own_inv
    scaled = grad_float * ln_gain
    parts = total[:, width + packed : width + packed + 4]
    first_total = parts[:, 0] + parts[:, 2]
    second_total = parts[:, 1] + parts[:, 3]
    grad_inputs = (
        own_inv * (scaled - first_total[:, None] / D - own_hat * (second_total[:, None] / D))
    ).astype(bf16)
    feature_rows = (
        lax.dynamic_slice_in_dim(all_stacked, lax.axis_index(gx) * sub_width, sub_width, axis=1)
        .reshape(-1, local + extra_rows, sub_width)[:, :local]
        .reshape(-1, sub_width)
    )
    grad_weight = lax.dot_general(
        feature_rows, portion, (((0,), (0,)), ((), ())), preferred_element_type=f32
    ).astype(bf16)
    return (grad_inputs, grad_weight, grad_up_bias, grad_ln_gain, grad_ln_bias)


def solution(mesh):
    cube = Mesh(mesh.devices.reshape(4, 2, 2, 4, 8), ("y", "core", "zh", "x", "gz"))
    return jax.shard_map(
        shards,
        mesh=cube,
        in_specs=(
            P(("y", "core", "gz"), gy),
            P(gy),
            P(gy),
            P(("zh", "x", "y", "core"), "gz"),
            P("gz"),
            P(("y", "core", "zh", "x"), "gz"),
        ),
        out_specs=(
            P(("y", "core", "gz"), gy),
            P(("zh", "x", "y", "core"), "gz"),
            P("gz"),
            P(gy),
            P(gy),
        ),
        check_vma=False,
    )
```

```python
import math

import jax
import jax.numpy as jnp
from jax import lax
from jax.sharding import Mesh, PartitionSpec as P

D = 12288


gelu_scale = math.sqrt(2.0 / math.pi)
cubic = 0.044715
epsilon = 1e-05

gx = ("y", "core")
gy = ("zh", "x")


def gelu_slope(value):
    inner = gelu_scale * (value + cubic * value * value * value)
    tangent = jnp.tanh(inner)
    return 0.5 * (1.0 + tangent) + 0.5 * value * (1.0 - tangent * tangent) * gelu_scale * (
        1.0 + 3.0 * cubic * value * value
    )


def exchange(blocks, axis):
    return lax.all_to_all(blocks, axis, split_axis=0, concat_axis=0, tiled=True)


def spread(block, axis):
    count = lax.axis_size(axis)
    return exchange(jnp.broadcast_to(block[None], (count,) + block.shape), axis)


def swap(block):
    return lax.ppermute(block, "zh", [(0, 1), (1, 0)])


def split_float(value):
    high = lax.reduce_precision(value, 8, 7)
    return high, value - high


def shards(inputs, ln_gain, ln_bias, weight_in, up_bias, grad_hidden):
    f32, bf16 = jnp.float32, jnp.bfloat16
    rows, width = inputs.shape
    hidden_width = weight_in.shape[1]
    sub_width = weight_in.shape[0]
    depth = lax.axis_size("gz")
    halves, around = lax.axis_size("zh"), lax.axis_size("x")
    local = depth * rows

    weight = lax.all_gather(weight_in, gx, axis=0, tiled=True)

    x_float = (
        spread(inputs, "gz")
        .reshape(halves, around, rows, width)
        .transpose(1, 0, 2, 3)
        .reshape(local, width)
        .astype(f32)
    )
    own_mean = jnp.mean(x_float, axis=1)
    own_centered = x_float - own_mean[:, None]
    own_square = jnp.sum(own_centered * own_centered, axis=1)
    late_cotangent = grad_hidden + (0.0 * x_float[0, 0]).astype(bf16)
    other_cotangent = swap(late_cotangent)
    moments = spread(jnp.stack([own_mean, own_square]), gy)
    mean = jnp.mean(moments[:, 0], axis=0)
    shift = moments[:, 0] - mean
    shift = shift + 0.0 * other_cotangent[0, 0].astype(f32)
    variance = (jnp.sum(moments[:, 1], axis=0) + width * jnp.sum(shift * shift, axis=0)) / D
    inv_std = lax.rsqrt(variance + epsilon)
    x_hat = (x_float - mean[:, None]) * inv_std[:, None]
    normed = (x_hat * ln_gain + ln_bias).astype(bf16)

    upper = lax.axis_index("zh") == 1
    cotangent = jnp.concatenate(
        [
            jnp.where(upper, other_cotangent, grad_hidden),
            jnp.where(upper, grad_hidden, other_cotangent),
        ]
    ).astype(f32)

    extra_rows = 8
    block = halves * rows
    affine = jnp.stack([*split_float(ln_gain), *split_float(ln_bias)]).astype(bf16)
    stacked = jnp.concatenate([normed, jnp.pad(affine, ((0, extra_rows - 4), (0, 0)))])
    all_stacked = lax.all_gather(stacked, gx, axis=0, tiled=True)
    partial_hidden = jnp.dot(stacked, weight, preferred_element_type=f32).astype(bf16)
    affine_parts = partial_hidden[local : local + 4].astype(f32)
    affine_parts = (affine_parts[0::2] + affine_parts[1::2]).astype(bf16)
    share = 2 * hidden_width // block
    affine_parts = jnp.pad(affine_parts.reshape(block, share), ((0, 0), (0, -share % 128)))
    arrived = exchange(
        jnp.concatenate(
            [
                partial_hidden[:local].reshape(around, block, hidden_width),
                jnp.broadcast_to(affine_parts[None], (around,) + affine_parts.shape),
            ],
            axis=2,
        ),
        "x",
    )
    half_sum = lax.reduce_precision(jnp.sum(arrived.astype(f32), axis=0), 8, 7)
    products = half_sum + swap(half_sum.astype(bf16)).astype(f32)
    product = products[:, :hidden_width]
    affine_product = products[:, hidden_width : hidden_width + share].reshape(2, hidden_width)
    grad_pre = (cotangent * gelu_slope(product + up_bias)).astype(bf16)
    grad_pre_float = grad_pre.astype(f32)
    token_sums = jnp.stack(
        [
            jnp.sum(grad_pre_float * affine_product[0], axis=1),
            jnp.sum(grad_pre_float * (product - affine_product[1]), axis=1),
        ],
        axis=1,
    )
    token_columns = jnp.concatenate(split_float(token_sums), axis=1).astype(bf16)
    around_rows = spread(
        jnp.concatenate([grad_pre, jnp.pad(token_columns, ((0, 0), (0, 124)))], axis=1), "x"
    )
    grad_local = around_rows[:, :, :hidden_width].reshape(local, hidden_width)
    token_parts = (
        around_rows[:, :, hidden_width : hidden_width + 4]
        .reshape(around, halves, rows, 4)
        .transpose(1, 0, 2, 3)
        .reshape(depth, rows, 4)
    )

    portion = lax.all_gather(grad_local, gx, axis=0, tiled=True)

    back = lax.dot_general(
        grad_local, weight, (((1,), (1,)), ((), ())), preferred_element_type=f32
    )
    sums = jnp.stack([jnp.sum(back * x_hat, axis=0), jnp.sum(back, axis=0)]).astype(bf16)
    packed = 2 * width // rows
    padding = -(packed + 4) % 128
    ordered = (
        back.astype(bf16)
        .reshape(around, halves, rows, width)
        .transpose(1, 0, 2, 3)
        .reshape(depth, rows, width)
    )
    landed = exchange(
        jnp.concatenate(
            [
                ordered,
                jnp.broadcast_to(sums.reshape(1, rows, packed), (depth, rows, packed)),
                token_parts,
                jnp.zeros((depth, rows, padding), bf16),
            ],
            axis=2,
        ),
        "gz",
    )
    total = jnp.sum(landed.astype(f32), axis=0)
    grad_float = total[:, :width].astype(bf16).astype(f32)
    small = jnp.concatenate(
        [
            total[:, width : width + packed].reshape(2 * width),
            jnp.sum(grad_local.astype(f32), axis=0),
        ]
    ).reshape(-1, 128)
    small_parts = spread(small, gx)

    def mine(value):
        ordered = value.reshape(around, halves, rows).transpose(1, 0, 2).reshape(depth, rows)
        return lax.dynamic_index_in_dim(ordered, lax.axis_index("gz"), 0, keepdims=False)[:, None]

    own_inv = mine(inv_std)
    own_hat = (inputs.astype(f32) - mine(mean)) * own_inv
    scaled = grad_float * ln_gain
    parts = total[:, width + packed : width + packed + 4]
    first_total = parts[:, 0] + parts[:, 2]
    second_total = parts[:, 1] + parts[:, 3]
    grad_inputs = (
        own_inv * (scaled - first_total[:, None] / D - own_hat * (second_total[:, None] / D))
    ).astype(bf16)
    feature_rows = (
        lax.dynamic_slice_in_dim(all_stacked, lax.axis_index(gx) * sub_width, sub_width, axis=1)
        .reshape(-1, local + extra_rows, sub_width)[:, :local]
        .reshape(-1, sub_width)
    )
    grad_weight = lax.dot_general(
        feature_rows, portion, (((0,), (0,)), ((), ())), preferred_element_type=f32
    ).astype(bf16)
    tie = 0.0 * grad_weight[0, 0].astype(f32)
    small = jnp.sum(small_parts + tie, axis=0).reshape(-1)
    grad_ln_gain, grad_ln_bias = small[:width], small[width : 2 * width]
    grad_up_bias = small[2 * width :]
    return (grad_inputs, grad_weight, grad_up_bias, grad_ln_gain, grad_ln_bias)


def solution(mesh):
    cube = Mesh(mesh.devices.reshape(4, 2, 2, 4, 8), ("y", "core", "zh", "x", "gz"))
    return jax.shard_map(
        shards,
        mesh=cube,
        in_specs=(
            P(("y", "core", "gz"), gy),
            P(gy),
            P(gy),
            P(("zh", "x", "y", "core"), "gz"),
            P("gz"),
            P(("y", "core", "zh", "x"), "gz"),
        ),
        out_specs=(
            P(("y", "core", "gz"), gy),
            P(("zh", "x", "y", "core"), "gz"),
            P("gz"),
            P(gy),
            P(gy),
        ),
        check_vma=False,
    )
```

```python
import math

import jax
import jax.numpy as jnp
from jax import lax
from jax.sharding import Mesh, PartitionSpec as P

D = 12288


gelu_scale = math.sqrt(2.0 / math.pi)
cubic = 0.044715
epsilon = 1e-05

gx = ("y", "core")
gy = ("zh", "x")


def gelu_slope(value):
    inner = gelu_scale * (value + cubic * value * value * value)
    tangent = jnp.tanh(inner)
    return 0.5 * (1.0 + tangent) + 0.5 * value * (1.0 - tangent * tangent) * gelu_scale * (
        1.0 + 3.0 * cubic * value * value
    )


def exchange(blocks, axis):
    return lax.all_to_all(blocks, axis, split_axis=0, concat_axis=0, tiled=True)


def spread(block, axis):
    count = lax.axis_size(axis)
    return exchange(jnp.broadcast_to(block[None], (count,) + block.shape), axis)


def swap(block):
    return lax.ppermute(block, "zh", [(0, 1), (1, 0)])


def split_float(value):
    high = lax.reduce_precision(value, 8, 7)
    return high, value - high


def shards(inputs, ln_gain, ln_bias, weight_in, up_bias, grad_hidden):
    f32, bf16 = jnp.float32, jnp.bfloat16
    rows, width = inputs.shape
    hidden_width = weight_in.shape[1]
    sub_width = weight_in.shape[0]
    depth = lax.axis_size("gz")
    halves, around = lax.axis_size("zh"), lax.axis_size("x")
    local = depth * rows

    weight = lax.all_gather(weight_in, gx, axis=0, tiled=True)

    x_float = (
        spread(inputs, "gz")
        .reshape(halves, around, rows, width)
        .transpose(1, 0, 2, 3)
        .reshape(local, width)
        .astype(f32)
    )
    own_mean = jnp.mean(x_float, axis=1)
    own_centered = x_float - own_mean[:, None]
    own_square = jnp.sum(own_centered * own_centered, axis=1)
    late_cotangent = grad_hidden + (0.0 * x_float[0, 0]).astype(bf16)
    other_cotangent = swap(late_cotangent)
    moments = spread(jnp.stack([own_mean, own_square]), gy)
    mean = jnp.mean(moments[:, 0], axis=0)
    shift = moments[:, 0] - mean
    variance = (jnp.sum(moments[:, 1], axis=0) + width * jnp.sum(shift * shift, axis=0)) / D
    inv_std = lax.rsqrt(variance + epsilon)
    x_hat = (x_float - mean[:, None]) * inv_std[:, None]
    normed = (x_hat * ln_gain + ln_bias).astype(bf16)

    upper = lax.axis_index("zh") == 1
    cotangent = jnp.concatenate(
        [
            jnp.where(upper, other_cotangent, grad_hidden),
            jnp.where(upper, grad_hidden, other_cotangent),
        ]
    ).astype(f32)

    extra_rows = 8
    block = halves * rows
    affine = jnp.stack([*split_float(ln_gain), *split_float(ln_bias)]).astype(bf16)
    stacked = jnp.concatenate([normed, jnp.pad(affine, ((0, extra_rows - 4), (0, 0)))])
    all_stacked = lax.all_gather(stacked, gx, axis=0, tiled=True)
    partial_hidden = jnp.dot(stacked, weight, preferred_element_type=f32).astype(bf16)
    affine_parts = partial_hidden[local : local + 4].astype(f32)
    affine_parts = affine_parts[0::2] + affine_parts[1::2]
    affine_parts = (affine_parts + 0.0 * other_cotangent[0, 0].astype(f32)).astype(bf16)
    share = 2 * hidden_width // block
    affine_parts = jnp.pad(affine_parts.reshape(block, share), ((0, 0), (0, -share % 128)))
    arrived = exchange(
        jnp.concatenate(
            [
                partial_hidden[:local].reshape(around, block, hidden_width),
                jnp.broadcast_to(affine_parts[None], (around,) + affine_parts.shape),
            ],
            axis=2,
        ),
        "x",
    )
    half_sum = lax.reduce_precision(jnp.sum(arrived.astype(f32), axis=0), 8, 7)
    products = half_sum + swap(half_sum.astype(bf16)).astype(f32)
    product = products[:, :hidden_width]
    affine_product = products[:, hidden_width : hidden_width + share].reshape(2, hidden_width)
    grad_pre = (cotangent * gelu_slope(product + up_bias)).astype(bf16)
    grad_pre_float = grad_pre.astype(f32)
    token_sums = jnp.stack(
        [
            jnp.sum(grad_pre_float * affine_product[0], axis=1),
            jnp.sum(grad_pre_float * (product - affine_product[1]), axis=1),
        ],
        axis=1,
    )
    token_columns = jnp.concatenate(split_float(token_sums), axis=1).astype(bf16)
    around_rows = spread(
        jnp.concatenate([grad_pre, jnp.pad(token_columns, ((0, 0), (0, 124)))], axis=1), "x"
    )
    grad_local = around_rows[:, :, :hidden_width].reshape(local, hidden_width)
    token_parts = (
        around_rows[:, :, hidden_width : hidden_width + 4]
        .reshape(around, halves, rows, 4)
        .transpose(1, 0, 2, 3)
        .reshape(depth, rows, 4)
    )

    portion = lax.all_gather(grad_local, gx, axis=0, tiled=True)

    back = lax.dot_general(
        grad_local, weight, (((1,), (1,)), ((), ())), preferred_element_type=f32
    )
    sums = jnp.stack([jnp.sum(back * x_hat, axis=0), jnp.sum(back, axis=0)]).astype(bf16)
    packed = 2 * width // rows
    padding = -(packed + 4) % 128
    ordered = (
        back.astype(bf16)
        .reshape(around, halves, rows, width)
        .transpose(1, 0, 2, 3)
        .reshape(depth, rows, width)
    )
    landed = exchange(
        jnp.concatenate(
            [
                ordered,
                jnp.broadcast_to(sums.reshape(1, rows, packed), (depth, rows, packed)),
                token_parts,
                jnp.zeros((depth, rows, padding), bf16),
            ],
            axis=2,
        ),
        "gz",
    )
    total = jnp.sum(landed.astype(f32), axis=0)
    grad_float = total[:, :width].astype(bf16).astype(f32)
    small = jnp.concatenate(
        [
            total[:, width : width + packed].reshape(2 * width),
            jnp.sum(grad_local.astype(f32), axis=0),
        ]
    ).reshape(-1, 128)
    small_parts = spread(small, gx)

    def mine(value):
        ordered = value.reshape(around, halves, rows).transpose(1, 0, 2).reshape(depth, rows)
        return lax.dynamic_index_in_dim(ordered, lax.axis_index("gz"), 0, keepdims=False)[:, None]

    own_inv = mine(inv_std)
    own_hat = (inputs.astype(f32) - mine(mean)) * own_inv
    scaled = grad_float * ln_gain
    parts = total[:, width + packed : width + packed + 4]
    first_total = parts[:, 0] + parts[:, 2]
    second_total = parts[:, 1] + parts[:, 3]
    grad_inputs = (
        own_inv * (scaled - first_total[:, None] / D - own_hat * (second_total[:, None] / D))
    ).astype(bf16)
    feature_rows = (
        lax.dynamic_slice_in_dim(all_stacked, lax.axis_index(gx) * sub_width, sub_width, axis=1)
        .reshape(-1, local + extra_rows, sub_width)[:, :local]
        .reshape(-1, sub_width)
    )
    grad_weight = lax.dot_general(
        feature_rows, portion, (((0,), (0,)), ((), ())), preferred_element_type=f32
    ).astype(bf16)
    tie = 0.0 * grad_weight[0, 0].astype(f32)
    small = jnp.sum(small_parts + tie, axis=0).reshape(-1)
    grad_ln_gain, grad_ln_bias = small[:width], small[width : 2 * width]
    grad_up_bias = small[2 * width :]
    return (grad_inputs, grad_weight, grad_up_bias, grad_ln_gain, grad_ln_bias)


def solution(mesh):
    cube = Mesh(mesh.devices.reshape(4, 2, 2, 4, 8), ("y", "core", "zh", "x", "gz"))
    return jax.shard_map(
        shards,
        mesh=cube,
        in_specs=(
            P(("y", "core", "gz"), gy),
            P(gy),
            P(gy),
            P(("zh", "x", "y", "core"), "gz"),
            P("gz"),
            P(("y", "core", "zh", "x"), "gz"),
        ),
        out_specs=(
            P(("y", "core", "gz"), gy),
            P(("zh", "x", "y", "core"), "gz"),
            P("gz"),
            P(gy),
            P(gy),
        ),
        check_vma=False,
    )
```
